32 devices in a mesh: slides: 1, row: 16 (over z, y, x), col: 2 (over core).
Axes of the slice: x: 2, y: 2, z: 4, core: 2. Of those that a mesh axis runs over, the one named last changes fastest.
Arguments:
- image: bfloat16 [64, 128, 768], P(('slides', 'row'), 'col'), may hold values from -6 to 6
- dw_kernel: float32 [49, 768], replicated, may hold values from -0.875 to 0.875
- w_in: bfloat16 [768, 3072], replicated, may hold values from -0.21875 to 0.21875
- w_out: bfloat16 [3072, 768], replicated, may hold values from -0.109375 to 0.109375
- layer_scale: float32 [768], replicated, may hold values from 0.5 to 1.5
- region_ids: int32 [32, 64], P(('slides', 'row'), 'col'), may hold values from 0 to 127, as said below
- region_slot: int32 [128], P('slides'), may hold values from 0 to 127, each once
- pool_grad: bfloat16 [128, 768], P(('slides', 'row', 'col')), may hold values from -6 to 6
Outputs:
- region_pool: float32 [128, 768], P(('slides', 'row', 'col'))
- grad_image: bfloat16 [64, 128, 768], P(('slides', 'row'), 'col')
- grad_w_in: float32 [768, 3072], P('slides', ('row', 'col'))
- grad_w_out: float32 [3072, 768], P(('slides', 'row', 'col'))
- grad_kernel: float32 [49, 768], P('slides')
The draws below stay inside these ranges and needn't reach their ends.
Inputs may be any that keep to these rules, and one draw needn't show every extreme that they name: `region_ids`: every region is named by some tile. `region_slot`: each slot once; slot s lies on index s // 4 of row+col.
All inputs are finite; a program needn't handle non-finite values.
Results may differ from the reference program's by a relative error of at most 0.007.
Values may be sent and summed in bfloat16 or wider, within the bound.
A program may use at most 192 MiB of HBM per device.

```python
import math
import jax
import jax.numpy as jnp
from jax import lax

C = 768
FF = 3072
ROWS = 64
COLS = 128
REGIONS = 128


def draw_region_ids(key, part):
    first, second, third = jax.random.split(key, 3)
    total = ROWS // 2 * (COLS // 2)
    lower = jax.random.randint(first, (total,), 0, REGIONS)
    upper = jax.random.randint(second, (total,), 0, REGIONS)
    order = jax.random.permutation(third, REGIONS).astype(jnp.int32)
    labels = order[jnp.minimum(lower, upper)]
    labels = labels.at[:REGIONS].set(order)
    return labels.reshape(ROWS // 2, COLS // 2).astype(jnp.int32)


def levels(key, shape, cuts, low, high):
    gain, own = 1.0, jax.random.fold_in(key, 6)
    for position, parts in cuts:
        heights = jnp.exp(jax.random.uniform(jax.random.fold_in(own, position), (parts,), jnp.float32, low / len(cuts), high / len(cuts)))
        gain = gain * jnp.repeat(heights, shape[position] // parts).reshape([-1 if axis == position else 1 for axis in range(len(shape))])
    return gain


def noise(stream_key, extent, spread, most, cuts=(), kind=jnp.bfloat16):
    loudness = levels(stream_key, extent, cuts, -0.22, 0.18) if cuts else 1.0
    entries = jax.random.normal(stream_key, extent, jnp.float32) * spread * loudness
    return jnp.minimum(jnp.maximum(entries, -most), most).astype(kind)


def setup_inputs(seed: int = 0, part: int = 0) -> dict:
    seeds = jax.random.split(jax.random.key(seed), 9)
    part_keys = jax.random.split(jax.random.fold_in(seeds[8], part), 9)
    image = noise(part_keys[0], (ROWS, COLS, C), 1.0, 6.0, ((0, 16), (1, 2)))
    dw_kernel = noise(seeds[1], (49, C), 49 ** -0.5, 0.875, (), jnp.float32)
    w_in = noise(seeds[2], (C, FF), C ** -0.5, 0.21875)
    w_out = noise(seeds[3], (FF, C), FF ** -0.5, 0.109375)
    layer_scale = jnp.clip(jax.random.uniform(seeds[4], (C,), jnp.float32, 0.5, 1.5), 0.5, 1.5)
    region_ids = draw_region_ids(jax.random.fold_in(jax.random.fold_in(seeds[8], part), 71), part)
    region_slot = jax.random.permutation(part_keys[6], REGIONS).astype(jnp.int32)
    pool_grad = noise(part_keys[7], (REGIONS, C), 1.0, 6.0, ((0, 32),))
    return {"image": image, "dw_kernel": dw_kernel, "w_in": w_in, "w_out": w_out, "layer_scale": layer_scale, "region_ids": region_ids, "region_slot": region_slot, "pool_grad": pool_grad}


def reference(image, dw_kernel, w_in, w_out, layer_scale, region_ids, region_slot, pool_grad):
    height, breadth, width = image.shape
    taps = dw_kernel.reshape(7, 7, width)
    xfull = image.astype(jnp.float32)
    xpad = jnp.pad(xfull, ((3, 3), (3, 3), (0, 0)))
    conv = jnp.zeros((height, breadth, width), jnp.float32)
    for a in range(7):
        for b in range(7):
            conv = conv + xpad[a:a + height, b:b + breadth] * taps[a, b]
    centre = conv - lax.optimization_barrier(jnp.mean(conv, axis=-1, keepdims=True))
    inv_std = lax.rsqrt(lax.optimization_barrier(jnp.mean(centre * centre, axis=-1, keepdims=True)) + 1e-06)
    normed_f = centre * inv_std
    normed = normed_f.astype(jnp.bfloat16).reshape(-1, width)
    pre = jnp.dot(normed, w_in, preferred_element_type=jnp.float32)
    hidden = jax.nn.gelu(pre, approximate=False).astype(jnp.bfloat16)
    branch = jnp.dot(hidden, w_out, preferred_element_type=jnp.float32).reshape(height, breadth, width)
    block = (xfull + layer_scale * branch).astype(jnp.bfloat16)
    tile_sum = block.astype(jnp.float32).reshape(height // 2, 2, breadth // 2, 2, width).sum(axis=(1, 3)).reshape(-1, width)
    slots = region_slot[region_ids.reshape(-1)].astype(jnp.int32)
    region_sum = jax.ops.segment_sum(tile_sum, slots, REGIONS)
    count = jax.ops.segment_sum(jnp.ones(slots.shape, jnp.float32), slots, REGIONS)
    region_pool = region_sum / (4.0 * count)[:, None]
    region_grad = (pool_grad.astype(jnp.float32) / (4.0 * count)[:, None]).astype(jnp.bfloat16)
    tile_grad = region_grad[slots].astype(jnp.float32).reshape(height // 2, 1, breadth // 2, 1, width)
    dblock = jnp.broadcast_to(tile_grad, (height // 2, 2, breadth // 2, 2, width)).reshape(height, breadth, width)
    g_out = (dblock * layer_scale).astype(jnp.bfloat16).reshape(-1, width)
    grad_w_out = jnp.dot(hidden.T, g_out, preferred_element_type=jnp.float32)
    dhidden = jnp.dot(g_out, w_out.T, preferred_element_type=jnp.float32)
    cdf = 0.5 * (1.0 + lax.erf(pre / math.sqrt(2.0)))
    density = jnp.exp(-0.5 * pre * pre) / math.sqrt(2.0 * math.pi)
    g_in = (dhidden * (cdf + pre * density)).astype(jnp.bfloat16)
    grad_w_in = jnp.dot(normed.T, g_in, preferred_element_type=jnp.float32)
    dnorm = jnp.dot(g_in, w_in.T, preferred_element_type=jnp.float32).reshape(height, breadth, width)
    dconv = inv_std * (dnorm - lax.optimization_barrier(jnp.mean(dnorm, axis=-1, keepdims=True)) - normed_f * lax.optimization_barrier(jnp.mean(dnorm * normed_f, axis=-1, keepdims=True)))
    dpad = jnp.pad(dconv, ((3, 3), (3, 3), (0, 0)))
    back = jnp.zeros((height, breadth, width), jnp.float32)
    kernel_rows = []
    for a in range(7):
        for b in range(7):
            back = back + dpad[6 - a:6 - a + height, 6 - b:6 - b + breadth] * taps[a, b]
            kernel_rows.append(lax.optimization_barrier(jnp.sum(xpad[a:a + height, b:b + breadth] * dconv, axis=(0, 1))))
    grad_kernel = jnp.stack(kernel_rows, axis=0)
    grad_image = (dblock + back).astype(jnp.bfloat16)
    return (region_pool, grad_image, grad_w_in, grad_w_out, grad_kernel)
```

```python
import functools
import math

import jax
import jax.numpy as jnp
from jax import lax
from jax.experimental import pallas as pl
from jax.experimental.pallas import tpu as pltpu
from jax.sharding import PartitionSpec as P

MESH = pl.DeviceIdType.MESH
EDGE = 16


def log2(count):
    bits = count.bit_length() - 1
    assert 1 << bits == count
    return bits


def bit(value, k):
    return lax.rem(lax.div(value, 1 << k), 2)


def place(index):
    return {"row": lax.div(index, 2), "col": lax.rem(index, 2)}


class Halo:
    def __init__(self, src, up, down, side, send, recv, row, col, rows):
        self.has_up, self.has_down = row > 0, row < rows - 1
        h, w = src.shape[0], src.shape[1]
        above, below = jnp.maximum(row - 1, 0), jnp.minimum(row + 1, rows - 1)
        cols = pl.ds(pl.multiple_of((1 - col) * (w - EDGE), EDGE), EDGE)
        last, first = pl.ds(h - 3, 3), pl.ds(0, 3)

        def copy(k, s, d, r, c):
            return pltpu.make_async_remote_copy(
                src_ref=s, dst_ref=d, send_sem=send.at[k], recv_sem=recv.at[k],
                device_id={"row": r, "col": c}, device_id_type=MESH,
            )

        self.up, self.down, self.side = up, down, side
        self.to_down = [
            copy(0, src.at[last], up, below, col),
            copy(1, src.at[last, cols], side.at[pl.ds(0, 3)], below, 1 - col),
        ]
        self.to_up = [
            copy(2, src.at[first], down, above, col),
            copy(3, src.at[first, cols], side.at[pl.ds(h + 3, 3)], above, 1 - col),
        ]
        self.across = copy(4, src.at[:, cols], side.at[pl.ds(3, h)], row, 1 - col)
        self.h = h
        self.targets = (above, below, row, col)

    def greet(self, barrier):
        above, below, row, col = self.targets
        pl.semaphore_signal(barrier, inc=1, device_id={"row": row, "col": 1 - col}, device_id_type=MESH)

        @pl.when(self.has_up)
        def _():
            for c in (col, 1 - col):
                pl.semaphore_signal(barrier, inc=1, device_id={"row": above, "col": c}, device_id_type=MESH)

        @pl.when(self.has_down)
        def _():
            for c in (col, 1 - col):
                pl.semaphore_signal(barrier, inc=1, device_id={"row": below, "col": c}, device_id_type=MESH)

        return 1 + 2 * self.has_up.astype(jnp.int32) + 2 * self.has_down.astype(jnp.int32)

    def start(self):
        self.across.start()

        @pl.when(self.has_down)
        def _():
            for c in self.to_down:
                c.start()

        @pl.when(self.has_up)
        def _():
            for c in self.to_up:
                c.start()

        @pl.when(jnp.logical_not(self.has_up))
        def _():
            self.up[...] = jnp.zeros_like(self.up)
            self.side[0:3] = jnp.zeros((3,) + self.side.shape[1:], self.side.dtype)

        @pl.when(jnp.logical_not(self.has_down))
        def _():
            self.down[...] = jnp.zeros_like(self.down)
            self.side[self.h + 3 : self.h + 6] = jnp.zeros((3,) + self.side.shape[1:], self.side.dtype)

    def finish(self):
        self.across.wait_send()
        self.across.wait_recv()

        @pl.when(self.has_down)
        def _():
            for c in self.to_down:
                c.wait_send()
            for c in self.to_up:
                c.wait_recv()

        @pl.when(self.has_up)
        def _():
            for c in self.to_up:
                c.wait_send()
            for c in self.to_down:
                c.wait_recv()


def gather_step(buf, send, recv, me, k):
    size = 1 << k
    start = lax.div(me, size) * size
    other = me + size * (1 - 2 * bit(me, k))
    return pltpu.make_async_remote_copy(
        src_ref=buf.at[pl.ds(start, size)], dst_ref=buf.at[pl.ds(start, size)],
        send_sem=send.at[k], recv_sem=recv.at[k],
        device_id=place(other), device_id_type=MESH,
    )


def greet_partners(barrier, me, levels):
    for k in range(levels):
        other = me + (1 << k) * (1 - 2 * bit(me, k))
        pl.semaphore_signal(barrier, inc=1, device_id=place(other), device_id_type=MESH)
    return levels


def opening(rows, src, msg, up, down, side, every, hs, hr, gs, gr):
    row, col = lax.axis_index("row"), lax.axis_index("col")
    me = row * 2 + col
    levels = log2(rows * 2)
    halo = Halo(src, up, down, side, hs, hr, row, col, rows)
    barrier = pltpu.get_barrier_semaphore()
    amount = halo.greet(barrier) + greet_partners(barrier, me, levels)
    pl.semaphore_wait(barrier, amount)
    every[me] = msg[...]
    halo.start()
    for k in range(levels):
        step = gather_step(every, gs, gr, me, k)
        step.start()
        step.wait_send()
        step.wait_recv()
    halo.finish()


def closing(rows, kr, slots, wi, ht, ex, src, wi_out, ht_out, ex_out, every, up, down, side,
            wi_in, ht_in, ex_in, wi_acc, ht_acc, ex_acc, wi_buf, ht_buf, ex_buf,
            s0, r0, ss, rs, hs, hr, gs, gr):
    row, col = lax.axis_index("row"), lax.axis_index("col")
    me = row * 2 + col
    levels = log2(rows * 2)
    nb = levels - 1
    halo = Halo(src, up, down, side, hs, hr, row, col, rows)
    barrier = pltpu.get_barrier_semaphore()
    amount = halo.greet(barrier) + greet_partners(barrier, me, levels)
    pl.semaphore_wait(barrier, amount)

    def order(p):
        head = list(range(nb - 1))
        p = p % max(nb - 1, 1)
        return head[p:] + head[:p] + [nb - 1]

    third = wi.shape[3] // 3
    parts = [
        (ex, ex_in, ex_acc, ex_buf, ex_out, pl.ds(0, ex.shape[3]), order(2)),
        (wi, wi_in, wi_acc, wi_buf, wi_out, pl.ds(0, third), order(0)),
        (wi, wi_in, wi_acc, wi_buf, wi_out, pl.ds(third, third), order(1)),
        (wi, wi_in, wi_acc, wi_buf, wi_out, pl.ds(2 * third, third), order(2)),
        (ht, ht_in, ht_acc, ht_buf, ht_out, pl.ds(0, ht.shape[3]), order(0)),
    ]
    swaps = []
    for p, (full, landed, _, _, _, lanes, _) in enumerate(parts):
        swap = pltpu.make_async_remote_copy(
            src_ref=full.at[:, 1 - col, :, lanes], dst_ref=landed.at[:, :, lanes],
            send_sem=s0.at[p], recv_sem=r0.at[p],
            device_id={"row": row, "col": 1 - col}, device_id_type=MESH,
        )
        swap.start()
        swaps.append(swap)
    halo.start()
    mine = [bit(row, k) for k in range(nb)]

    def combos(bits):
        return [[(b, (j >> i) & 1) for i, b in enumerate(bits)] for j in range(1 << len(bits))]

    def step(p, s, free, make=True):
        _, _, acc, buf, _, lanes, bits = parts[p]
        b = bits[s]
        partner = row + (1 << b) * (1 - 2 * mine[b])
        away = (1 - mine[b]) * (1 << b)
        for done in bits[:s]:
            away = away + mine[done] * (1 << done)
        rest = bits[s + 1 :]
        value = dict(free)
        slot = (1 << nb) - (1 << (nb - s))
        for i, f in enumerate(rest):
            away = away + value[f] * (1 << f)
            slot = slot + value[f] * (1 << i)
        home = away + (2 * mine[b] - 1) * (1 << b)
        if not make:
            return None, home, slot
        copy = pltpu.make_async_remote_copy(
            src_ref=acc.at[away, :, lanes], dst_ref=buf.at[slot, :, lanes],
            send_sem=ss.at[p, slot], recv_sem=rs.at[p, slot],
            device_id={"row": partner, "col": col}, device_id_type=MESH,
        )
        return copy, home, slot

    for p, (full, landed, acc, _, _, lanes, bits) in enumerate(parts):
        swaps[p].wait_recv()
        for first in (1, 0):
            for free in combos(bits[1:]):
                copy, home, _ = step(p, 0, free, bool(first))
                b = bits[0]
                at = home - (2 * mine[b] - 1) * (1 << b) if first else home
                acc[at, :, lanes] = (
                    full[at, col, :, lanes].astype(jnp.float32) + landed[at, :, lanes].astype(jnp.float32)
                ).astype(acc.dtype)
                if first:
                    copy.start()
    for s in range(nb):
        for p, (_, _, acc, buf, out, lanes, bits) in enumerate(parts):
            rest = bits[s + 1 :]
            if not rest:
                copy, home, slot = step(p, s, [])
                copy.wait_recv()
                out[:, lanes] = acc[home, :, lanes].astype(jnp.float32) + buf[slot, :, lanes].astype(jnp.float32)
                continue
            b = rest[0]
            for first in (1, 0):
                for free in combos(rest[1:]):
                    now = free + [(b, 1 - mine[b] if first else mine[b])]
                    copy, home, slot = step(p, s, now)
                    copy.wait_recv()
                    acc[home, :, lanes] = (
                        acc[home, :, lanes].astype(jnp.float32) + buf[slot, :, lanes].astype(jnp.float32)
                    ).astype(acc.dtype)
                    if first:
                        onward, _, _ = step(p, s + 1, free)
                        onward.start()
    chunks = ex.shape[3] // 128
    own = [ex_out[slots : slots + kr, 128 * i : 128 * i + 128] for i in range(chunks)]
    pad = every.shape[1] - kr * chunks
    if pad:
        own.append(jnp.zeros((pad, 128), jnp.float32))
    every[me] = jnp.concatenate(own, axis=0)
    for k in range(levels):
        hop = gather_step(every, gs, gr, me, k)
        hop.start()
        hop.wait_send()
        hop.wait_recv()
    halo.finish()
    for p, (_, _, _, _, _, _, bits) in enumerate(parts):
        swaps[p].wait_send()
        for s in range(nb):
            for free in combos(bits[s + 1 :]):
                step(p, s, free)[0].wait_send()


def halo_shapes(h, w, c):
    return (
        jax.ShapeDtypeStruct((3, w, c), jnp.bfloat16),
        jax.ShapeDtypeStruct((3, w, c), jnp.bfloat16),
        jax.ShapeDtypeStruct((h + 6, EDGE, c), jnp.bfloat16),
    )


def joined(block, up, down, side, col):
    centre = jnp.concatenate([up, block, down], axis=0)
    zero = jnp.zeros_like(side[:, :3])
    left = jnp.where(col == 1, side[:, EDGE - 3 :], zero)
    right = jnp.where(col == 0, side[:, :3], zero)
    return jnp.concatenate([left, centre, right], axis=1)


def depthwise(padded, taps, height, breadth, flipped):
    total = jnp.zeros((height, breadth, padded.shape[2]), jnp.float32)
    for a in range(7):
        if flipped:
            terms = [
                padded[6 - a : 6 - a + height, 6 - b : 6 - b + breadth] * taps[a, b]
                for b in range(7)
            ]
        else:
            terms = [padded[a : a + height, b : b + breadth] * taps[a, b] for b in range(7)]
        row_total = terms[0]
        for term in terms[1:]:
            row_total = row_total + term
        total = total + row_total
    return total


VMEM = pl.BlockSpec(memory_space=pltpu.VMEM)
DMA = pltpu.SemaphoreType.DMA


def shards(image, dw_kernel, w_in, w_out, layer_scale, region_ids, region_slot, pool_grad):
    height, breadth, width = image.shape
    rows, cols = lax.axis_size("row"), lax.axis_size("col")
    assert cols == 2
    n = rows * cols
    levels = log2(n)
    row, col = lax.axis_index("row"), lax.axis_index("col")
    me = row * 2 + col
    taps = dw_kernel.reshape(7, 7, width)
    regions = region_slot.shape[0]
    slots = pool_grad.shape[0]
    hidden_width = w_in.shape[1]

    labels = region_ids.reshape(-1)
    region_iota = jnp.arange(regions, dtype=jnp.int32)
    id_onehot = (labels[:, None] == region_iota[None, :]).astype(jnp.bfloat16)
    slot_onehot = (region_slot[:, None] == region_iota[None, :]).astype(jnp.bfloat16)
    tile_onehot = jnp.dot(id_onehot, slot_onehot, preferred_element_type=jnp.float32)
    local_count = jnp.sum(tile_onehot, axis=0)
    payload = jnp.concatenate([pool_grad.reshape(-1), local_count.astype(jnp.bfloat16)])
    height16 = -(-payload.shape[0] // (256 * 16)) * 16
    message = jnp.pad(payload, (0, height16 * 256 - payload.shape[0])).reshape(height16, 256)

    up, down, side, every = pl.pallas_call(
        functools.partial(opening, rows),
        out_shape=halo_shapes(height, breadth, width)
        + (jax.ShapeDtypeStruct((n, height16, 256), jnp.bfloat16),),
        in_specs=[VMEM] * 2,
        out_specs=(VMEM,) * 4,
        scratch_shapes=[DMA((5,)), DMA((5,)), DMA((levels,)), DMA((levels,))],
        compiler_params=pltpu.CompilerParams(
            collective_id=0, has_side_effects=True, vmem_limit_bytes=16 << 20
        ),
        name="opening",
    )(image, message)
    flat = every.reshape(n, -1)
    every_pool = flat[:, : slots * width].reshape(regions, width)
    count = jnp.sum(flat[:, slots * width : slots * width + regions].astype(jnp.float32), axis=0)
    region_grad = (every_pool.astype(jnp.float32) / (4.0 * count)[:, None]).astype(jnp.bfloat16)

    pos_onehot = jnp.broadcast_to(
        tile_onehot.astype(jnp.bfloat16).reshape(height // 2, 1, breadth // 2, 1, regions),
        (height // 2, 2, breadth // 2, 2, regions),
    ).reshape(-1, regions)

    xfull = image.astype(jnp.float32)
    xpad = joined(image, up, down, side, col).astype(jnp.float32)
    conv = depthwise(xpad, taps, height, breadth, False)
    centre = conv - jnp.mean(conv, axis=-1, keepdims=True)
    inv_std = lax.rsqrt(jnp.mean(centre * centre, axis=-1, keepdims=True) + 1e-06)
    normed_f = centre * inv_std
    normed = normed_f.astype(jnp.bfloat16).reshape(-1, width)
    pre = jnp.dot(normed, w_in, preferred_element_type=jnp.float32)
    cdf = 0.5 * (1.0 + lax.erf(pre / math.sqrt(2.0)))
    hidden = (pre * cdf).astype(jnp.bfloat16)
    branch = jnp.dot(hidden, w_out, preferred_element_type=jnp.float32).reshape(
        height, breadth, width
    )
    block = (xfull + layer_scale * branch).astype(jnp.bfloat16).reshape(-1, width)
    first = (((0,), (0,)), ((), ()))
    partial_sum = lax.dot_general(pos_onehot, block, first, preferred_element_type=jnp.float32)

    dblock = jnp.dot(pos_onehot, region_grad, preferred_element_type=jnp.float32)
    g_out = (dblock * layer_scale).astype(jnp.bfloat16)
    dblock = dblock.reshape(height, breadth, width)
    dhidden = jnp.dot(g_out, w_out.T, preferred_element_type=jnp.float32)
    density = jnp.exp(-0.5 * pre * pre) / math.sqrt(2.0 * math.pi)
    g_in = (dhidden * (cdf + pre * density)).astype(jnp.bfloat16)
    part_in = lax.dot_general(g_in, normed, first, preferred_element_type=jnp.float32)
    part_hid = lax.dot_general(hidden, pos_onehot, first, preferred_element_type=jnp.float32)
    dnorm = jnp.dot(g_in, w_in.T, preferred_element_type=jnp.float32).reshape(
        height, breadth, width
    )
    dconv = inv_std * (
        dnorm
        - jnp.mean(dnorm, axis=-1, keepdims=True)
        - normed_f * jnp.mean(dnorm * normed_f, axis=-1, keepdims=True)
    )
    kernel_rows = []
    for a in range(7):
        for b in range(7):
            kernel_rows.append(jnp.sum(xpad[a : a + height, b : b + breadth] * dconv, axis=(0, 1)))
    kr = -(-49 // n)
    part_kernel = jnp.pad(jnp.stack(kernel_rows, axis=0), ((0, kr * n - 49), (0, 0)))

    depth = hidden_width // n
    wi = part_in.astype(jnp.bfloat16).reshape(rows, 2, depth, width)
    ht = part_hid.astype(jnp.bfloat16).reshape(rows, 2, depth, regions)
    tall = -(-(slots + kr) // 16) * 16
    ex = jnp.concatenate(
        [
            partial_sum.reshape(n, slots, width),
            part_kernel.reshape(n, kr, width),
            jnp.zeros((n, tall - slots - kr, width), jnp.float32),
        ],
        axis=1,
    ).astype(jnp.bfloat16).reshape(rows, 2, tall, width)
    dconv_b = dconv.astype(jnp.bfloat16)
    ktall = -(-(kr * width // 128) // 8) * 8
    f32 = jnp.float32
    b16 = jnp.bfloat16

    def three(lead):
        return [
            pltpu.VMEM((lead, depth, width), b16),
            pltpu.VMEM((lead, depth, regions), b16),
            pltpu.VMEM((lead, tall, width), b16),
        ]

    wi_sum, ht_sum, ex_sum, every_kernel, up, down, side = pl.pallas_call(
        functools.partial(closing, rows, kr, slots),
        out_shape=(
            jax.ShapeDtypeStruct((depth, width), f32),
            jax.ShapeDtypeStruct((depth, regions), f32),
            jax.ShapeDtypeStruct((tall, width), f32),
            jax.ShapeDtypeStruct((n, ktall, 128), f32),
        )
        + halo_shapes(height, breadth, width),
        in_specs=[VMEM] * 4,
        out_specs=(VMEM,) * 7,
        scratch_shapes=three(rows) + three(rows) + three(rows)
        + [DMA((5,)), DMA((5,)), DMA((5, rows)), DMA((5, rows)),
           DMA((5,)), DMA((5,)), DMA((levels,)), DMA((levels,))],
        compiler_params=pltpu.CompilerParams(
            collective_id=1, has_side_effects=True, vmem_limit_bytes=56 << 20
        ),
        name="closing",
    )(wi, ht, ex, dconv_b)

    own_count = lax.dynamic_slice_in_dim(count, me * slots, slots)
    region_pool = ex_sum[:slots] / (4.0 * own_count)[:, None]
    grad_w_in = wi_sum.T
    scaled = (region_grad.astype(f32) * layer_scale).astype(b16).astype(f32)
    grad_w_out = jnp.dot(ht_sum, scaled, precision=lax.Precision.HIGHEST, preferred_element_type=f32)
    chunks = width // 128
    grad_kernel = (
        every_kernel[:, : kr * chunks]
        .reshape(n, chunks, kr, 128)
        .transpose(0, 2, 1, 3)
        .reshape(n * kr, width)[:49]
    )
    dpad = joined(dconv_b, up, down, side, col).astype(f32)
    back = depthwise(dpad, taps, height, breadth, True)
    grad_image = (dblock + back).astype(b16)
    return (region_pool, grad_image, grad_w_in, grad_w_out, grad_kernel)


def solution(mesh):
    placed = (
        P(("slides", "row"), "col", None),
        P(),
        P(),
        P(),
        P(),
        P(("slides", "row"), "col"),
        P("slides"),
        P(("slides", "row", "col"), None),
    )
    return jax.shard_map(
        shards,
        mesh=mesh,
        in_specs=placed,
        out_specs=(
            P(("slides", "row", "col"), None),
            P(("slides", "row"), "col", None),
            P("slides", ("row", "col")),
            P(("slides", "row", "col"), None),
            P("slides", None),
        ),
        check_vma=False,
    )
```

```python
import functools
import math

import jax
import jax.numpy as jnp
from jax import lax
from jax.experimental import pallas as pl
from jax.experimental.pallas import tpu as pltpu
from jax.sharding import PartitionSpec as P

MESH = pl.DeviceIdType.MESH
EDGE = 16


def log2(count):
    bits = count.bit_length() - 1
    assert 1 << bits == count
    return bits


def bit(value, k):
    return lax.rem(lax.div(value, 1 << k), 2)


class Halo:
    def __init__(self, src, up, down, side, send, recv, row, col, rows):
        self.has_up, self.has_down = row > 0, row < rows - 1
        h, w = src.shape[0], src.shape[1]
        above, below = jnp.maximum(row - 1, 0), jnp.minimum(row + 1, rows - 1)
        cols = pl.ds(pl.multiple_of((1 - col) * (w - EDGE), EDGE), EDGE)
        last, first = pl.ds(h - 3, 3), pl.ds(0, 3)

        def copy(k, s, d, r, c):
            return pltpu.make_async_remote_copy(
                src_ref=s, dst_ref=d, send_sem=send.at[k], recv_sem=recv.at[k],
                device_id={"row": r, "col": c}, device_id_type=MESH,
            )

        self.up, self.down, self.side = up, down, side
        self.to_down = [
            copy(0, src.at[last], up, below, col),
            copy(1, src.at[last, cols], side.at[pl.ds(0, 3)], below, 1 - col),
        ]
        self.to_up = [
            copy(2, src.at[first], down, above, col),
            copy(3, src.at[first, cols], side.at[pl.ds(h + 3, 3)], above, 1 - col),
        ]
        self.across = copy(4, src.at[:, cols], side.at[pl.ds(3, h)], row, 1 - col)
        self.h = h
        self.targets = (above, below, row, col)

    def greet(self, barrier):
        above, below, row, col = self.targets
        pl.semaphore_signal(barrier, inc=1, device_id={"row": row, "col": 1 - col}, device_id_type=MESH)

        @pl.when(self.has_up)
        def _():
            for c in (col, 1 - col):
                pl.semaphore_signal(barrier, inc=1, device_id={"row": above, "col": c}, device_id_type=MESH)

        @pl.when(self.has_down)
        def _():
            for c in (col, 1 - col):
                pl.semaphore_signal(barrier, inc=1, device_id={"row": below, "col": c}, device_id_type=MESH)

        return 1 + 2 * self.has_up.astype(jnp.int32) + 2 * self.has_down.astype(jnp.int32)

    def start(self):
        self.across.start()

        @pl.when(self.has_down)
        def _():
            for c in self.to_down:
                c.start()

        @pl.when(self.has_up)
        def _():
            for c in self.to_up:
                c.start()

        @pl.when(jnp.logical_not(self.has_up))
        def _():
            self.up[...] = jnp.zeros_like(self.up)
            self.side[0:3] = jnp.zeros((3,) + self.side.shape[1:], self.side.dtype)

        @pl.when(jnp.logical_not(self.has_down))
        def _():
            self.down[...] = jnp.zeros_like(self.down)
            self.side[self.h + 3 : self.h + 6] = jnp.zeros((3,) + self.side.shape[1:], self.side.dtype)

    def finish(self):
        self.across.wait_send()
        self.across.wait_recv()

        @pl.when(self.has_down)
        def _():
            for c in self.to_down:
                c.wait_send()
            for c in self.to_up:
                c.wait_recv()

        @pl.when(self.has_up)
        def _():
            for c in self.to_up:
                c.wait_send()
            for c in self.to_down:
                c.wait_recv()


def hop(src, dst, send, recv, row, col):
    return pltpu.make_async_remote_copy(
        src_ref=src, dst_ref=dst, send_sem=send, recv_sem=recv,
        device_id={"row": row, "col": col}, device_id_type=MESH,
    )


def ahead(row, offset, rows):
    return lax.rem(row + offset, rows)


def greet_rows(barrier, row, col, rows):
    for o in range(1, rows):
        pl.semaphore_signal(
            barrier, inc=1, device_id={"row": ahead(row, o, rows), "col": col}, device_id_type=MESH
        )
    return rows - 1


def spread(buf, row, col, rows, send, recv):
    own = buf.at[row, col]
    return [
        hop(own, own, send.at[o], recv.at[o], ahead(row, o, rows), col) for o in range(1, rows)
    ]


def share(buf, row, col, send, recv):
    half = buf.at[:, col]
    return hop(half, half, send.at[0], recv.at[0], row, 1 - col)


def opening(rows, src, msg, up, down, side, every, hs, hr, gs, gr):
    row, col = lax.axis_index("row"), lax.axis_index("col")
    halo = Halo(src, up, down, side, hs, hr, row, col, rows)
    barrier = pltpu.get_barrier_semaphore()
    amount = halo.greet(barrier) + greet_rows(barrier, row, col, rows)
    every[row, col] = msg[...]
    pl.semaphore_wait(barrier, amount)
    copies = spread(every, row, col, rows, gs, gr)
    for copy in copies:
        copy.start()
    halo.start()
    for copy in copies:
        copy.wait_recv()
    last = share(every, row, col, gs, gr)
    last.start()
    halo.finish()
    last.wait_recv()
    for copy in copies + [last]:
        copy.wait_send()


def closing(rows, skip, wi, ht, ex, src, wi_out, ht_out, ex_out, every, up, down, side,
            wi_in, ht_in, ex_in, wi_acc, ht_acc, ex_acc, wi_buf, ht_buf, ex_buf,
            s0, r0, ss, rs, hs, hr, es, er, gs, gr):
    row, col = lax.axis_index("row"), lax.axis_index("col")
    nb = log2(rows)
    f32 = jnp.float32
    halo = Halo(src, up, down, side, hs, hr, row, col, rows)
    barrier = pltpu.get_barrier_semaphore()
    amount = halo.greet(barrier) + greet_rows(barrier, row, col, rows)
    pl.semaphore_wait(barrier, amount)

    def order(p):
        head = list(range(nb - 1))
        head = head[::-1] if p < 0 else head[p:] + head[:p]
        return head + [nb - 1]

    third = wi.shape[3] // 3
    parts = [
        (wi, wi_in, wi_acc, wi_buf, wi_out, pl.ds(0, third), order(2)),
        (wi, wi_in, wi_acc, wi_buf, wi_out, pl.ds(third, third), order(1)),
        (wi, wi_in, wi_acc, wi_buf, wi_out, pl.ds(2 * third, third), order(-1)),
        (ht, ht_in, ht_acc, ht_buf, ht_out, pl.ds(0, ht.shape[3]), order(0)),
    ]
    extra = hop(ex.at[:, 1 - col], ex_in, s0.at[len(parts)], r0.at[len(parts)], row, 1 - col)
    extra.start()
    swaps = []
    for p, (full, landed, _, _, _, lanes, _) in enumerate(parts):
        swap = hop(
            full.at[:, 1 - col, :, lanes], landed.at[:, :, lanes], s0.at[p], r0.at[p], row, 1 - col
        )
        swap.start()
        swaps.append(swap)
    mine = [bit(row, k) for k in range(nb)]

    def combos(bits):
        return [[(b, (j >> i) & 1) for i, b in enumerate(bits)] for j in range(1 << len(bits))]

    def step(p, s, free, make=True):
        _, _, acc, buf, _, lanes, bits = parts[p]
        b = bits[s]
        partner = row + (1 << b) * (1 - 2 * mine[b])
        away = (1 - mine[b]) * (1 << b)
        for done in bits[:s]:
            away = away + mine[done] * (1 << done)
        rest = bits[s + 1 :]
        value = dict(free)
        slot = (1 << nb) - (1 << (nb - s))
        for i, f in enumerate(rest):
            away = away + value[f] * (1 << f)
            slot = slot + value[f] * (1 << i)
        home = away + (2 * mine[b] - 1) * (1 << b)
        if not make:
            return None, home, slot
        copy = hop(
            acc.at[away, :, lanes], buf.at[slot, :, lanes], ss.at[p, slot], rs.at[p, slot],
            partner, col,
        )
        return copy, home, slot

    for p, (full, landed, acc, _, _, lanes, bits) in enumerate(parts):
        swaps[p].wait_recv()
        for first in (1, 0):
            for free in combos(bits[1:]):
                copy, home, _ = step(p, 0, free, bool(first))
                b = bits[0]
                at = home - (2 * mine[b] - 1) * (1 << b) if first else home
                acc[at, :, lanes] = (
                    full[at, col, :, lanes].astype(f32) + landed[at, :, lanes].astype(f32)
                ).astype(acc.dtype)
                if first:
                    copy.start()
        if p == 0:
            extra.wait_recv()
            for r in range(rows):
                ex_acc[r] = (ex[r, col].astype(f32) + ex_in[r].astype(f32)).astype(ex_acc.dtype)
            tosses = []
            for o in range(1, rows):
                to = ahead(row, o, rows)
                toss = hop(ex_acc.at[to], ex_buf.at[o], es.at[o], er.at[o], to, col)
                toss.start()
                tosses.append(toss)
            halo.start()
    copies = spread(every, row, col, rows, gs, gr)
    last = share(every, row, col, gs, gr)
    for s in range(nb):
        for p, (_, _, acc, buf, out, lanes, bits) in enumerate(parts):
            rest = bits[s + 1 :]
            if not rest:
                copy, home, slot = step(p, s, [])
                copy.wait_recv()
                out[:, lanes] = acc[home, :, lanes].astype(f32) + buf[slot, :, lanes].astype(f32)
                continue
            b = rest[0]
            for first in (1, 0):
                for free in combos(rest[1:]):
                    now = free + [(b, 1 - mine[b] if first else mine[b])]
                    copy, home, slot = step(p, s, now)
                    copy.wait_recv()
                    acc[home, :, lanes] = (
                        acc[home, :, lanes].astype(f32) + buf[slot, :, lanes].astype(f32)
                    ).astype(acc.dtype)
                    if first:
                        onward, _, _ = step(p, s + 1, free)
                        onward.start()
        if s == 0:
            total = ex_acc[row].astype(f32)
            for o in range(1, rows):
                tosses[o - 1].wait_recv()
                total = total + ex_buf[o].astype(f32)
            ex_out[...] = total
            every[row, col] = total[skip : skip + every.shape[2]]
            for copy in copies:
                copy.start()
        if s == nb - 2:
            for copy in copies:
                copy.wait_recv()
            last.start()
    halo.finish()
    last.wait_recv()
    for copy in copies + tosses + [last, extra]:
        copy.wait_send()
    for p, (_, _, _, _, _, _, bits) in enumerate(parts):
        swaps[p].wait_send()
        for s in range(nb):
            for free in combos(bits[s + 1 :]):
                step(p, s, free)[0].wait_send()


def halo_shapes(h, w, c):
    return (
        jax.ShapeDtypeStruct((3, w, c), jnp.bfloat16),
        jax.ShapeDtypeStruct((3, w, c), jnp.bfloat16),
        jax.ShapeDtypeStruct((h + 6, EDGE, c), jnp.bfloat16),
    )


def joined(block, up, down, side, col):
    centre = jnp.concatenate([up, block, down], axis=0)
    zero = jnp.zeros_like(side[:, :3])
    left = jnp.where(col == 1, side[:, EDGE - 3 :], zero)
    right = jnp.where(col == 0, side[:, :3], zero)
    return jnp.concatenate([left, centre, right], axis=1)


def depthwise(padded, taps, height, breadth, flipped):
    total = jnp.zeros((height, breadth, padded.shape[2]), jnp.float32)
    for a in range(7):
        if flipped:
            terms = [
                padded[6 - a : 6 - a + height, 6 - b : 6 - b + breadth] * taps[a, b]
                for b in range(7)
            ]
        else:
            terms = [padded[a : a + height, b : b + breadth] * taps[a, b] for b in range(7)]
        row_total = terms[0]
        for term in terms[1:]:
            row_total = row_total + term
        total = total + row_total
    return total


VMEM = pl.BlockSpec(memory_space=pltpu.VMEM)
DMA = pltpu.SemaphoreType.DMA


def shards(image, dw_kernel, w_in, w_out, layer_scale, region_ids, region_slot, pool_grad):
    height, breadth, width = image.shape
    rows, cols = lax.axis_size("row"), lax.axis_size("col")
    assert cols == 2
    n = rows * cols
    row, col = lax.axis_index("row"), lax.axis_index("col")
    me = row * 2 + col
    taps = dw_kernel.reshape(7, 7, width)
    regions = region_slot.shape[0]
    slots = pool_grad.shape[0]
    hidden_width = w_in.shape[1]

    labels = region_ids.reshape(-1)
    region_iota = jnp.arange(regions, dtype=jnp.int32)
    id_onehot = (labels[:, None] == region_iota[None, :]).astype(jnp.bfloat16)
    slot_onehot = (region_slot[:, None] == region_iota[None, :]).astype(jnp.bfloat16)
    tile_onehot = jnp.dot(id_onehot, slot_onehot, preferred_element_type=jnp.float32)
    local_count = jnp.sum(tile_onehot, axis=0)
    payload = jnp.concatenate([pool_grad.reshape(-1), local_count.astype(jnp.bfloat16)])
    height16 = -(-payload.shape[0] // (256 * 16)) * 16
    message = jnp.pad(payload, (0, height16 * 256 - payload.shape[0])).reshape(height16, 256)

    up, down, side, every = pl.pallas_call(
        functools.partial(opening, rows),
        out_shape=halo_shapes(height, breadth, width)
        + (jax.ShapeDtypeStruct((rows, 2, height16, 256), jnp.bfloat16),),
        in_specs=[VMEM] * 2,
        out_specs=(VMEM,) * 4,
        scratch_shapes=[DMA((5,)), DMA((5,)), DMA((rows,)), DMA((rows,))],
        compiler_params=pltpu.CompilerParams(
            collective_id=0, has_side_effects=True, vmem_limit_bytes=16 << 20
        ),
        name="opening",
    )(image, message)
    flat = every.reshape(n, -1)
    every_pool = flat[:, : slots * width].reshape(regions, width)
    count = jnp.sum(flat[:, slots * width : slots * width + regions].astype(jnp.float32), axis=0)
    region_grad = (every_pool.astype(jnp.float32) / (4.0 * count)[:, None]).astype(jnp.bfloat16)

    pos_onehot = jnp.broadcast_to(
        tile_onehot.astype(jnp.bfloat16).reshape(height // 2, 1, breadth // 2, 1, regions),
        (height // 2, 2, breadth // 2, 2, regions),
    ).reshape(-1, regions)

    xfull = image.astype(jnp.float32)
    xpad = joined(image, up, down, side, col).astype(jnp.float32)
    conv = depthwise(xpad, taps, height, breadth, False)
    centre = conv - jnp.mean(conv, axis=-1, keepdims=True)
    inv_std = lax.rsqrt(jnp.mean(centre * centre, axis=-1, keepdims=True) + 1e-06)
    normed_f = centre * inv_std
    normed = normed_f.astype(jnp.bfloat16).reshape(-1, width)
    pre = jnp.dot(normed, w_in, preferred_element_type=jnp.float32)
    cdf = 0.5 * (1.0 + lax.erf(pre / math.sqrt(2.0)))
    hidden = (pre * cdf).astype(jnp.bfloat16)
    branch = jnp.dot(hidden, w_out, preferred_element_type=jnp.float32).reshape(
        height, breadth, width
    )
    block = (xfull + layer_scale * branch).astype(jnp.bfloat16).reshape(-1, width)
    first = (((0,), (0,)), ((), ()))
    partial_sum = lax.dot_general(pos_onehot, block, first, preferred_element_type=jnp.float32)

    dblock = jnp.dot(pos_onehot, region_grad, preferred_element_type=jnp.float32)
    g_out = (dblock * layer_scale).astype(jnp.bfloat16)
    dblock = dblock.reshape(height, breadth, width)
    dhidden = jnp.dot(g_out, w_out.T, preferred_element_type=jnp.float32)
    density = jnp.exp(-0.5 * pre * pre) / math.sqrt(2.0 * math.pi)
    g_in = (dhidden * (cdf + pre * density)).astype(jnp.bfloat16)
    part_in = lax.dot_general(g_in, normed, first, preferred_element_type=jnp.float32)
    part_hid = lax.dot_general(hidden, pos_onehot, first, preferred_element_type=jnp.float32)
    dnorm = jnp.dot(g_in, w_in.T, preferred_element_type=jnp.float32).reshape(
        height, breadth, width
    )
    dconv = inv_std * (
        dnorm
        - jnp.mean(dnorm, axis=-1, keepdims=True)
        - normed_f * jnp.mean(dnorm * normed_f, axis=-1, keepdims=True)
    )
    kernel_rows = []
    for a in range(7):
        for b in range(7):
            kernel_rows.append(jnp.sum(xpad[a : a + height, b : b + breadth] * dconv, axis=(0, 1)))
    kr = -(-49 // n)
    part_kernel = jnp.pad(jnp.stack(kernel_rows, axis=0), ((0, kr * n - 49), (0, 0)))

    depth = hidden_width // n
    wi = part_in.astype(jnp.bfloat16).reshape(rows, 2, depth, width)
    ht = part_hid.astype(jnp.bfloat16).reshape(rows, 2, depth, regions)
    lanes = 384
    skip, keep = slots * width // lanes, kr * width // lanes
    tall = -(-(skip + 8) // 16) * 16
    assert width % lanes == 0 and skip % 8 == 0 and keep <= 8
    ex = jnp.concatenate(
        [
            partial_sum.reshape(n, skip, lanes),
            part_kernel.reshape(n, keep, lanes),
            jnp.zeros((n, tall - skip - keep, lanes), jnp.float32),
        ],
        axis=1,
    ).astype(jnp.bfloat16).reshape(rows, 2, tall, lanes)
    dconv_b = dconv.astype(jnp.bfloat16)
    f32 = jnp.float32
    b16 = jnp.bfloat16

    def three(lead):
        return [
            pltpu.VMEM((lead, depth, width), b16),
            pltpu.VMEM((lead, depth, regions), b16),
            pltpu.VMEM((lead, tall, lanes), b16),
        ]

    wi_sum, ht_sum, ex_sum, every_kernel, up, down, side = pl.pallas_call(
        functools.partial(closing, rows, skip),
        out_shape=(
            jax.ShapeDtypeStruct((depth, width), f32),
            jax.ShapeDtypeStruct((depth, regions), f32),
            jax.ShapeDtypeStruct((tall, lanes), f32),
            jax.ShapeDtypeStruct((rows, 2, 8, lanes), f32),
        )
        + halo_shapes(height, breadth, width),
        in_specs=[VMEM] * 4,
        out_specs=(VMEM,) * 7,
        scratch_shapes=three(rows) + three(rows) + three(rows)
        + [DMA((5,)), DMA((5,)), DMA((4, rows)), DMA((4, rows)), DMA((5,)), DMA((5,)),
           DMA((rows,)), DMA((rows,)), DMA((rows,)), DMA((rows,))],
        compiler_params=pltpu.CompilerParams(
            collective_id=1, has_side_effects=True, vmem_limit_bytes=56 << 20
        ),
        name="closing",
    )(wi, ht, ex, dconv_b)

    own_count = lax.dynamic_slice_in_dim(count, me * slots, slots)
    region_pool = ex_sum[:skip].reshape(slots, width) / (4.0 * own_count)[:, None]
    grad_w_in = wi_sum.T
    scaled = (region_grad.astype(f32) * layer_scale).astype(b16).astype(f32)
    grad_w_out = jnp.dot(ht_sum, scaled, precision=lax.Precision.HIGHEST, preferred_element_type=f32)
    grad_kernel = every_kernel[:, :, :keep].reshape(n * kr, width)[:49]
    dpad = joined(dconv_b, up, down, side, col).astype(f32)
    back = depthwise(dpad, taps, height, breadth, True)
    grad_image = (dblock + back).astype(b16)
    return (region_pool, grad_image, grad_w_in, grad_w_out, grad_kernel)


def solution(mesh):
    placed = (
        P(("slides", "row"), "col", None),
        P(),
        P(),
        P(),
        P(),
        P(("slides", "row"), "col"),
        P("slides"),
        P(("slides", "row", "col"), None),
    )
    return jax.shard_map(
        shards,
        mesh=mesh,
        in_specs=placed,
        out_specs=(
            P(("slides", "row", "col"), None),
            P(("slides", "row"), "col", None),
            P("slides", ("row", "col")),
            P(("slides", "row", "col"), None),
            P("slides", None),
        ),
        check_vma=False,
    )
```

```python
import functools
import math

import jax
import jax.numpy as jnp
from jax import lax
from jax.experimental import pallas as pl
from jax.experimental.pallas import tpu as pltpu
from jax.sharding import PartitionSpec as P

MESH = pl.DeviceIdType.MESH
EDGE = 16


def log2(count):
    bits = count.bit_length() - 1
    assert 1 << bits == count
    return bits


def bit(value, k):
    return lax.rem(lax.div(value, 1 << k), 2)


class Halo:
    def __init__(self, src, up, down, side, send, recv, row, col, rows):
        self.has_up, self.has_down = row > 0, row < rows - 1
        h, w = src.shape[0], src.shape[1]
        above, below = jnp.maximum(row - 1, 0), jnp.minimum(row + 1, rows - 1)
        cols = pl.ds(pl.multiple_of((1 - col) * (w - EDGE), EDGE), EDGE)
        last, first = pl.ds(h - 3, 3), pl.ds(0, 3)

        def copy(k, s, d, r, c):
            return pltpu.make_async_remote_copy(
                src_ref=s, dst_ref=d, send_sem=send.at[k], recv_sem=recv.at[k],
                device_id={"row": r, "col": c}, device_id_type=MESH,
            )

        self.up, self.down, self.side = up, down, side
        self.to_down = [copy(0, src.at[last], up, below, col)]
        self.to_up = [copy(2, src.at[first], down, above, col)]
        self.corners = [
            copy(1, up.at[:, cols], side.at[pl.ds(0, 3)], row, 1 - col),
            copy(3, down.at[:, cols], side.at[pl.ds(h + 3, 3)], row, 1 - col),
        ]
        self.across = copy(4, src.at[:, cols], side.at[pl.ds(3, h)], row, 1 - col)
        self.h = h
        self.targets = (above, below, row, col)

    def greet(self, barrier):
        above, below, row, col = self.targets
        pl.semaphore_signal(barrier, inc=1, device_id={"row": row, "col": 1 - col}, device_id_type=MESH)

        @pl.when(self.has_up)
        def _():
            for c in (col, 1 - col):
                pl.semaphore_signal(barrier, inc=1, device_id={"row": above, "col": c}, device_id_type=MESH)

        @pl.when(self.has_down)
        def _():
            for c in (col, 1 - col):
                pl.semaphore_signal(barrier, inc=1, device_id={"row": below, "col": c}, device_id_type=MESH)

        return 1 + 2 * self.has_up.astype(jnp.int32) + 2 * self.has_down.astype(jnp.int32)

    def start(self):
        self.across.start()

        @pl.when(self.has_down)
        def _():
            for c in self.to_down:
                c.start()

        @pl.when(self.has_up)
        def _():
            for c in self.to_up:
                c.start()

        @pl.when(jnp.logical_not(self.has_up))
        def _():
            self.up[...] = jnp.zeros_like(self.up)

        @pl.when(jnp.logical_not(self.has_down))
        def _():
            self.down[...] = jnp.zeros_like(self.down)

    def relay(self):
        @pl.when(self.has_down)
        def _():
            for c in self.to_up:
                c.wait_recv()

        @pl.when(self.has_up)
        def _():
            for c in self.to_down:
                c.wait_recv()

        for c in self.corners:
            c.start()

    def finish(self):
        @pl.when(self.has_down)
        def _():
            for c in self.to_down:
                c.wait_send()

        @pl.when(self.has_up)
        def _():
            for c in self.to_up:
                c.wait_send()

        for c in [self.across] + self.corners:
            c.wait_send()
            c.wait_recv()


def hop(src, dst, send, recv, row, col):
    return pltpu.make_async_remote_copy(
        src_ref=src, dst_ref=dst, send_sem=send, recv_sem=recv,
        device_id={"row": row, "col": col}, device_id_type=MESH,
    )


def ahead(row, offset, rows):
    return lax.rem(row + offset, rows)


def greet_rows(barrier, row, col, rows):
    for o in range(1, rows):
        pl.semaphore_signal(
            barrier, inc=1, device_id={"row": ahead(row, o, rows), "col": col}, device_id_type=MESH
        )
    return rows - 1


def spread(buf, row, col, rows, send, recv):
    own = buf.at[row, col]
    return [
        hop(own, own, send.at[o], recv.at[o], ahead(row, o, rows), col) for o in range(1, rows)
    ]


def share(buf, row, col, send, recv):
    half = buf.at[:, col]
    return hop(half, half, send.at[0], recv.at[0], row, 1 - col)


def opening(rows, src, msg, up, down, side, every, hs, hr, gs, gr):
    row, col = lax.axis_index("row"), lax.axis_index("col")
    halo = Halo(src, up, down, side, hs, hr, row, col, rows)
    barrier = pltpu.get_barrier_semaphore()
    amount = halo.greet(barrier) + greet_rows(barrier, row, col, rows)
    every[row, col] = msg[...]
    pl.semaphore_wait(barrier, amount)
    copies = spread(every, row, col, rows, gs, gr)
    for copy in copies:
        copy.start()
    halo.start()
    for copy in copies:
        copy.wait_recv()
    last = share(every, row, col, gs, gr)
    last.start()
    halo.relay()
    halo.finish()
    last.wait_recv()
    for copy in copies + [last]:
        copy.wait_send()


def closing(rows, skip, wi, ht, ex, src, wi_out, ht_out, ex_out, every, up, down, side,
            wi_in, ht_in, ex_in, wi_acc, ht_acc, ex_acc, wi_buf, ht_buf, ex_buf,
            s0, r0, ss, rs, hs, hr, es, er, gs, gr):
    row, col = lax.axis_index("row"), lax.axis_index("col")
    nb = log2(rows)
    f32 = jnp.float32
    halo = Halo(src, up, down, side, hs, hr, row, col, rows)
    barrier = pltpu.get_barrier_semaphore()
    amount = halo.greet(barrier) + greet_rows(barrier, row, col, rows)
    pl.semaphore_wait(barrier, amount)

    def order(p):
        head = list(range(nb - 1))
        head = head[::-1] if p < 0 else head[p:] + head[:p]
        return head + [nb - 1]

    third = wi.shape[3] // 3
    parts = [
        (wi, wi_in, wi_acc, wi_buf, wi_out, pl.ds(0, third), order(2)),
        (wi, wi_in, wi_acc, wi_buf, wi_out, pl.ds(third, third), order(1)),
        (wi, wi_in, wi_acc, wi_buf, wi_out, pl.ds(2 * third, third), order(-1)),
        (ht, ht_in, ht_acc, ht_buf, ht_out, pl.ds(0, ht.shape[3]), order(0)),
    ]
    extra = hop(ex.at[:, 1 - col], ex_in, s0.at[len(parts)], r0.at[len(parts)], row, 1 - col)
    extra.start()
    swaps = []
    for p, (full, landed, _, _, _, lanes, _) in enumerate(parts):
        swap = hop(
            full.at[:, 1 - col, :, lanes], landed.at[:, :, lanes], s0.at[p], r0.at[p], row, 1 - col
        )
        swap.start()
        swaps.append(swap)
    mine = [bit(row, k) for k in range(nb)]

    def combos(bits):
        return [[(b, (j >> i) & 1) for i, b in enumerate(bits)] for j in range(1 << len(bits))]

    def step(p, s, free, make=True):
        _, _, acc, buf, _, lanes, bits = parts[p]
        b = bits[s]
        partner = row + (1 << b) * (1 - 2 * mine[b])
        away = (1 - mine[b]) * (1 << b)
        for done in bits[:s]:
            away = away + mine[done] * (1 << done)
        rest = bits[s + 1 :]
        value = dict(free)
        slot = (1 << nb) - (1 << (nb - s))
        for i, f in enumerate(rest):
            away = away + value[f] * (1 << f)
            slot = slot + value[f] * (1 << i)
        home = away + (2 * mine[b] - 1) * (1 << b)
        if not make:
            return None, home, slot
        copy = hop(
            acc.at[away, :, lanes], buf.at[slot, :, lanes], ss.at[p, slot], rs.at[p, slot],
            partner, col,
        )
        return copy, home, slot

    for p, (full, landed, acc, _, _, lanes, bits) in enumerate(parts):
        swaps[p].wait_recv()
        for first in (1, 0):
            for free in combos(bits[1:]):
                copy, home, _ = step(p, 0, free, bool(first))
                b = bits[0]
                at = home - (2 * mine[b] - 1) * (1 << b) if first else home
                acc[at, :, lanes] = (
                    full[at, col, :, lanes].astype(f32) + landed[at, :, lanes].astype(f32)
                ).astype(acc.dtype)
                if first:
                    copy.start()
        if p == 0:
            extra.wait_recv()
            for r in range(rows):
                ex_acc[r] = (ex[r, col].astype(f32) + ex_in[r].astype(f32)).astype(ex_acc.dtype)
            tosses = []
            for o in range(1, rows):
                to = ahead(row, o, rows)
                toss = hop(ex_acc.at[to], ex_buf.at[o], es.at[o], er.at[o], to, col)
                toss.start()
                tosses.append(toss)
            halo.start()
    copies = spread(every, row, col, rows, gs, gr)
    last = share(every, row, col, gs, gr)
    for s in range(nb):
        for p, (_, _, acc, buf, out, lanes, bits) in enumerate(parts):
            rest = bits[s + 1 :]
            if not rest:
                copy, home, slot = step(p, s, [])
                copy.wait_recv()
                out[:, lanes] = acc[home, :, lanes].astype(f32) + buf[slot, :, lanes].astype(f32)
                continue
            b = rest[0]
            for first in (1, 0):
                for free in combos(rest[1:]):
                    now = free + [(b, 1 - mine[b] if first else mine[b])]
                    copy, home, slot = step(p, s, now)
                    copy.wait_recv()
                    acc[home, :, lanes] = (
                        acc[home, :, lanes].astype(f32) + buf[slot, :, lanes].astype(f32)
                    ).astype(acc.dtype)
                    if first:
                        onward, _, _ = step(p, s + 1, free)
                        onward.start()
        if s == 0:
            total = ex_acc[row].astype(f32)
            for o in range(1, rows):
                tosses[o - 1].wait_recv()
                total = total + ex_buf[o].astype(f32)
            ex_out[...] = total
            every[row, col] = total[skip : skip + every.shape[2]]
            for copy in copies:
                copy.start()
        if s == nb - 2:
            for copy in copies:
                copy.wait_recv()
            last.start()
            halo.relay()
    halo.finish()
    last.wait_recv()
    for copy in copies + tosses + [last, extra]:
        copy.wait_send()
    for p, (_, _, _, _, _, _, bits) in enumerate(parts):
        swaps[p].wait_send()
        for s in range(nb):
            for free in combos(bits[s + 1 :]):
                step(p, s, free)[0].wait_send()


def halo_shapes(h, w, c):
    return (
        jax.ShapeDtypeStruct((3, w, c), jnp.bfloat16),
        jax.ShapeDtypeStruct((3, w, c), jnp.bfloat16),
        jax.ShapeDtypeStruct((h + 6, EDGE, c), jnp.bfloat16),
    )


def joined(block, up, down, side, col):
    centre = jnp.concatenate([up, block, down], axis=0)
    zero = jnp.zeros_like(side[:, :3])
    left = jnp.where(col == 1, side[:, EDGE - 3 :], zero)
    right = jnp.where(col == 0, side[:, :3], zero)
    return jnp.concatenate([left, centre, right], axis=1)


def depthwise(padded, taps, height, breadth, flipped):
    total = jnp.zeros((height, breadth, padded.shape[2]), jnp.float32)
    for a in range(7):
        if flipped:
            terms = [
                padded[6 - a : 6 - a + height, 6 - b : 6 - b + breadth] * taps[a, b]
                for b in range(7)
            ]
        else:
            terms = [padded[a : a + height, b : b + breadth] * taps[a, b] for b in range(7)]
        row_total = terms[0]
        for term in terms[1:]:
            row_total = row_total + term
        total = total + row_total
    return total


VMEM = pl.BlockSpec(memory_space=pltpu.VMEM)
DMA = pltpu.SemaphoreType.DMA


def shards(image, dw_kernel, w_in, w_out, layer_scale, region_ids, region_slot, pool_grad):
    height, breadth, width = image.shape
    rows, cols = lax.axis_size("row"), lax.axis_size("col")
    assert cols == 2
    n = rows * cols
    row, col = lax.axis_index("row"), lax.axis_index("col")
    me = row * 2 + col
    taps = dw_kernel.reshape(7, 7, width)
    regions = region_slot.shape[0]
    slots = pool_grad.shape[0]
    hidden_width = w_in.shape[1]

    labels = region_ids.reshape(-1)
    region_iota = jnp.arange(regions, dtype=jnp.int32)
    id_onehot = (labels[:, None] == region_iota[None, :]).astype(jnp.bfloat16)
    slot_onehot = (region_slot[:, None] == region_iota[None, :]).astype(jnp.bfloat16)
    tile_onehot = jnp.dot(id_onehot, slot_onehot, preferred_element_type=jnp.float32)
    local_count = jnp.sum(tile_onehot, axis=0)
    payload = jnp.concatenate([pool_grad.reshape(-1), local_count.astype(jnp.bfloat16)])
    height16 = -(-payload.shape[0] // (256 * 16)) * 16
    message = jnp.pad(payload, (0, height16 * 256 - payload.shape[0])).reshape(height16, 256)

    up, down, side, every = pl.pallas_call(
        functools.partial(opening, rows),
        out_shape=halo_shapes(height, breadth, width)
        + (jax.ShapeDtypeStruct((rows, 2, height16, 256), jnp.bfloat16),),
        in_specs=[VMEM] * 2,
        out_specs=(VMEM,) * 4,
        scratch_shapes=[DMA((5,)), DMA((5,)), DMA((rows,)), DMA((rows,))],
        compiler_params=pltpu.CompilerParams(
            collective_id=0, has_side_effects=True, vmem_limit_bytes=16 << 20
        ),
        name="opening",
    )(image, message)
    flat = every.reshape(n, -1)
    every_pool = flat[:, : slots * width].reshape(regions, width)
    count = jnp.sum(flat[:, slots * width : slots * width + regions].astype(jnp.float32), axis=0)
    region_grad = (every_pool.astype(jnp.float32) / (4.0 * count)[:, None]).astype(jnp.bfloat16)

    pos_onehot = jnp.broadcast_to(
        tile_onehot.astype(jnp.bfloat16).reshape(height // 2, 1, breadth // 2, 1, regions),
        (height // 2, 2, breadth // 2, 2, regions),
    ).reshape(-1, regions)

    xfull = image.astype(jnp.float32)
    xpad = joined(image, up, down, side, col).astype(jnp.float32)
    conv = depthwise(xpad, taps, height, breadth, False)
    centre = conv - jnp.mean(conv, axis=-1, keepdims=True)
    inv_std = lax.rsqrt(jnp.mean(centre * centre, axis=-1, keepdims=True) + 1e-06)
    normed_f = centre * inv_std
    normed = normed_f.astype(jnp.bfloat16).reshape(-1, width)
    pre = jnp.dot(normed, w_in, preferred_element_type=jnp.float32)
    cdf = 0.5 * (1.0 + lax.erf(pre / math.sqrt(2.0)))
    hidden = (pre * cdf).astype(jnp.bfloat16)
    branch = jnp.dot(hidden, w_out, preferred_element_type=jnp.float32).reshape(
        height, breadth, width
    )
    block = (xfull + layer_scale * branch).astype(jnp.bfloat16).reshape(-1, width)
    first = (((0,), (0,)), ((), ()))
    partial_sum = lax.dot_general(pos_onehot, block, first, preferred_element_type=jnp.float32)

    dblock = jnp.dot(pos_onehot, region_grad, preferred_element_type=jnp.float32)
    g_out = (dblock * layer_scale).astype(jnp.bfloat16)
    dblock = dblock.reshape(height, breadth, width)
    dhidden = jnp.dot(g_out, w_out.T, preferred_element_type=jnp.float32)
    density = jnp.exp(-0.5 * pre * pre) / math.sqrt(2.0 * math.pi)
    g_in = (dhidden * (cdf + pre * density)).astype(jnp.bfloat16)
    part_in = lax.dot_general(g_in, normed, first, preferred_element_type=jnp.float32)
    part_hid = lax.dot_general(hidden, pos_onehot, first, preferred_element_type=jnp.float32)
    dnorm = jnp.dot(g_in, w_in.T, preferred_element_type=jnp.float32).reshape(
        height, breadth, width
    )
    dconv = inv_std * (
        dnorm
        - jnp.mean(dnorm, axis=-1, keepdims=True)
        - normed_f * jnp.mean(dnorm * normed_f, axis=-1, keepdims=True)
    )
    kernel_rows = []
    for a in range(7):
        for b in range(7):
            kernel_rows.append(jnp.sum(xpad[a : a + height, b : b + breadth] * dconv, axis=(0, 1)))
    kr = -(-49 // n)
    part_kernel = jnp.pad(jnp.stack(kernel_rows, axis=0), ((0, kr * n - 49), (0, 0)))

    depth = hidden_width // n
    wi = part_in.astype(jnp.bfloat16).reshape(rows, 2, depth, width)
    ht = part_hid.astype(jnp.bfloat16).reshape(rows, 2, depth, regions)
    lanes = 384
    skip, keep = slots * width // lanes, kr * width // lanes
    tall = -(-(skip + 8) // 16) * 16
    assert width % lanes == 0 and skip % 8 == 0 and keep <= 8
    ex = jnp.concatenate(
        [
            partial_sum.reshape(n, skip, lanes),
            part_kernel.reshape(n, keep, lanes),
            jnp.zeros((n, tall - skip - keep, lanes), jnp.float32),
        ],
        axis=1,
    ).astype(jnp.bfloat16).reshape(rows, 2, tall, lanes)
    dconv_b = dconv.astype(jnp.bfloat16)
    f32 = jnp.float32
    b16 = jnp.bfloat16

    def three(lead):
        return [
            pltpu.VMEM((lead, depth, width), b16),
            pltpu.VMEM((lead, depth, regions), b16),
            pltpu.VMEM((lead, tall, lanes), b16),
        ]

    wi_sum, ht_sum, ex_sum, every_kernel, up, down, side = pl.pallas_call(
        functools.partial(closing, rows, skip),
        out_shape=(
            jax.ShapeDtypeStruct((depth, width), f32),
            jax.ShapeDtypeStruct((depth, regions), f32),
            jax.ShapeDtypeStruct((tall, lanes), f32),
            jax.ShapeDtypeStruct((rows, 2, 8, lanes), f32),
        )
        + halo_shapes(height, breadth, width),
        in_specs=[VMEM] * 4,
        out_specs=(VMEM,) * 7,
        scratch_shapes=three(rows) + three(rows) + three(rows)
        + [DMA((5,)), DMA((5,)), DMA((4, rows)), DMA((4, rows)), DMA((5,)), DMA((5,)),
           DMA((rows,)), DMA((rows,)), DMA((rows,)), DMA((rows,))],
        compiler_params=pltpu.CompilerParams(
            collective_id=1, has_side_effects=True, vmem_limit_bytes=56 << 20
        ),
        name="closing",
    )(wi, ht, ex, dconv_b)

    own_count = lax.dynamic_slice_in_dim(count, me * slots, slots)
    region_pool = ex_sum[:skip].reshape(slots, width) / (4.0 * own_count)[:, None]
    grad_w_in = wi_sum.T
    scaled = (region_grad.astype(f32) * layer_scale).astype(b16).astype(f32)
    grad_w_out = jnp.dot(ht_sum, scaled, precision=lax.Precision.HIGHEST, preferred_element_type=f32)
    grad_kernel = every_kernel[:, :, :keep].reshape(n * kr, width)[:49]
    dpad = joined(dconv_b, up, down, side, col).astype(f32)
    back = depthwise(dpad, taps, height, breadth, True)
    grad_image = (dblock + back).astype(b16)
    return (region_pool, grad_image, grad_w_in, grad_w_out, grad_kernel)


def solution(mesh):
    placed = (
        P(("slides", "row"), "col", None),
        P(),
        P(),
        P(),
        P(),
        P(("slides", "row"), "col"),
        P("slides"),
        P(("slides", "row", "col"), None),
    )
    return jax.shard_map(
        shards,
        mesh=mesh,
        in_specs=placed,
        out_specs=(
            P(("slides", "row", "col"), None),
            P(("slides", "row"), "col", None),
            P("slides", ("row", "col")),
            P(("slides", "row", "col"), None),
            P("slides", None),
        ),
        check_vma=False,
    )
```
